32 devices in a mesh: dp: 16 (over z, y, core), tensor: 2 (over x).
Axes of the slice: x: 2, y: 2, z: 4, core: 2. Of those that a mesh axis runs over, the one named last changes fastest.
Arguments:
- layer_inputs: bfloat16 [2048, 8192], P('dp', 'tensor'), may hold values from -6 to 6
- out_grads: bfloat16 [2048, 14336], P('dp', 'tensor'), may hold values from -0.125 to 0.125
- basis: float32 [8192, 512], P('tensor'), may hold values from -0.0625 to 0.0625
- first: float32 [512, 14336], P('dp', 'tensor'), may hold values from -3 to 3
- second: float32 [512, 14336], P('dp', 'tensor'), may hold values from 0.05 to 2
Outputs:
- new_basis: float32 [8192, 512], P('tensor')
- new_first: float32 [512, 14336], P('dp', 'tensor')
- new_second: float32 [512, 14336], P('dp', 'tensor')
- update: float32 [512, 14336], P('dp', 'tensor')
The draws below stay inside these ranges and needn't reach their ends.
All inputs are finite; a program needn't handle non-finite values.
Results may differ from the reference program's by a relative error of at most 0.0013.
The reference program's roundings to bfloat16 on the way (of `basis_low`, `scores`, `grad_low`, `backward`, `left_low` and `probe`) count: a program that leaves them out, or rounds other values in their place, can miss the bound.
Values may be sent and summed in bfloat16 or wider, within the bound.
A program may use at most 128 MiB of HBM per device.

```python
import math
import jax
import jax.numpy as jnp
from jax import lax

D = 8192
FF = 14336
RANK = 512
PI_STEPS = 6
TOKENS = 2048


def levels(key, shape, cuts, low, top_value):
    def one(dim, blocks):
        heights = jax.random.uniform(jax.random.fold_in(jax.random.fold_in(key, 6), dim), (blocks,), jnp.float32, low / len(cuts), top_value / len(cuts))
        return jnp.repeat(jnp.exp(heights), shape[dim] // blocks).reshape((-1,) + (1,) * (len(shape) - dim - 1))

    gain = one(*cuts[0])
    for cut in cuts[1:]:
        gain = gain * one(*cut)
    return gain


def bell_draw(own_key, dims, scale, most, split=(), kind=jnp.bfloat16):
    entries = jax.random.normal(own_key, dims, jnp.float32) * scale
    if len(split) > 0:
        entries = levels(own_key, dims, split, -0.22, 0.18) * entries
    return jnp.clip(entries, min=-most, max=most).astype(kind)


def setup_inputs(seed: int = 0) -> dict:
    keys = jax.random.split(jax.random.key(seed), 6)
    return {
        "layer_inputs": bell_draw(keys[0], (TOKENS, D), 1.0, 6.0, ((0, 16), (1, 2))),
        "out_grads": bell_draw(keys[1], (TOKENS, FF), TOKENS ** -0.5, 0.125, ((0, 16), (1, 2))),
        "basis": bell_draw(keys[2], (D, RANK), D ** -0.5, 0.0625, ((0, 2),), jnp.float32),
        "first": bell_draw(keys[3], (RANK, FF), 0.5, 3.0, ((0, 16), (1, 2)), jnp.float32),
        "second": jnp.clip(jnp.exp(math.log(2.0) - 3.6888794 * jax.random.uniform(keys[4], (RANK, FF), jnp.float32) ** levels(keys[4], (RANK, FF), ((0, 16), (1, 2)), -0.2, 0.2)), 0.05, 2.0),
    }


EXACT = lax.Precision.HIGHEST

def matmul(left, right):
    return jnp.dot(left, right, precision=EXACT, preferred_element_type=jnp.float32)

def leading(normed):
    rank_count = normed.shape[0]
    vector = jnp.ones((rank_count,), jnp.float32) / jnp.sqrt(jnp.float32(rank_count))
    for sweep in range(PI_STEPS):
        vector = matmul(normed, vector)
        vector = vector / jnp.sqrt(jnp.sum(vector * vector) + 1e-12)
    return vector

def reference(layer_inputs, out_grads, basis, first, second):
    basis_low = basis.astype(jnp.bfloat16)
    scores = jnp.dot(layer_inputs, basis_low, preferred_element_type=jnp.float32).astype(jnp.bfloat16)
    grad_proj = jnp.dot(scores.T, out_grads, preferred_element_type=jnp.float32)
    grad_low = grad_proj.astype(jnp.bfloat16)
    backward = jnp.dot(out_grads, grad_low.T, preferred_element_type=jnp.float32).astype(jnp.bfloat16)
    tangent = jnp.dot(layer_inputs.T, backward, preferred_element_type=jnp.float32)
    coupling = matmul(basis.T, tangent)
    resid = tangent - matmul(basis, coupling)
    kernel = matmul(resid.T, resid)
    total = jnp.trace(kernel)
    normed = kernel / total
    vector = leading(normed)
    ratio = jnp.sum(vector * matmul(normed, vector))
    theta = 4.0 * jnp.sqrt(ratio)
    sigma = jnp.sqrt(total * ratio + 1e-06)
    left_vec = matmul(resid, vector) / sigma
    cosine_val = jnp.cos(theta)
    sine_val = jnp.sin(theta)
    basis_dir = matmul(basis, vector)
    new_basis = basis + (cosine_val - 1.0) * jnp.outer(basis_dir, vector) + sine_val * jnp.outer(left_vec, vector)
    rotation = matmul(new_basis.T, basis)
    left_low = left_vec.astype(jnp.bfloat16)
    probe = jnp.dot(layer_inputs, left_low, preferred_element_type=jnp.float32).astype(jnp.bfloat16)
    along = jnp.dot(probe, out_grads, preferred_element_type=jnp.float32)
    lead_row = matmul(vector, grad_proj)
    grad_new = grad_proj + (cosine_val - 1.0) * jnp.outer(vector, lead_row) + sine_val * jnp.outer(vector, along)
    new_first = 0.9 * matmul(rotation, first) + 0.1 * grad_new
    new_second = 0.95 * matmul(rotation * rotation, second) + 0.05 * grad_new * grad_new
    update = new_first / (jnp.sqrt(new_second) + 1e-06)
    return (new_basis, new_first, new_second, update)
```

```python
import jax
import jax.numpy as jnp
from jax import lax
from jax.sharding import PartitionSpec as P

PI_STEPS = 6


EXACT = lax.Precision.HIGHEST


def matmul(left, right):
    return jnp.dot(left, right, precision=EXACT, preferred_element_type=jnp.float32)


def leading(normed):
    rank_count = normed.shape[0]
    vector = jnp.ones((rank_count,), jnp.float32) / jnp.sqrt(jnp.float32(rank_count))
    for sweep in range(PI_STEPS):
        vector = matmul(normed, vector)
        vector = vector / jnp.sqrt(jnp.sum(vector * vector) + 1e-12)
    return vector


def pair_sum(part, count):
    if count == 2:
        return part + lax.ppermute(part, "tensor", [(0, 1), (1, 0)])
    return lax.psum(part, "tensor")


def to_columns(block, count):
    rows, columns = block.shape
    pieces = block.reshape(rows, count, columns // count).transpose(1, 0, 2)
    pieces = lax.all_to_all(pieces, "dp", 0, 0, tiled=True)
    return pieces.reshape(count * rows, columns // count)


def body(dp, tensor, layer_inputs, out_grads, basis, first, second):
    rows_own = first.shape[0]
    rank = basis.shape[1]
    feats = basis.shape[0] // dp
    me = lax.axis_index("dp")

    grads_t = to_columns(out_grads, dp)
    basis_low = basis.astype(jnp.bfloat16)
    score_part = jnp.dot(layer_inputs, basis_low, preferred_element_type=jnp.float32)
    scores = pair_sum(score_part, tensor).astype(jnp.bfloat16)
    scores_all = lax.all_gather(scores, "dp", axis=0, tiled=True)
    inputs_t = to_columns(layer_inputs, dp)
    moments = jnp.stack([first, second]).reshape(2, rows_own, dp, -1).transpose(2, 0, 1, 3)
    moments = lax.all_to_all(moments, "dp", 0, 0, tiled=True)
    width = moments.shape[3]
    first_t = moments[:, 0].reshape(rank, width)
    second_t = moments[:, 1].reshape(rank, width)
    basis_own = lax.dynamic_slice_in_dim(basis, me * feats, feats, 0)

    grad_proj = jnp.dot(scores_all.T, grads_t, preferred_element_type=jnp.float32)
    grad_low = grad_proj.astype(jnp.bfloat16)
    back_part = jnp.dot(grads_t, grad_low.T, preferred_element_type=jnp.float32)
    back_own = lax.psum_scatter(back_part, "dp", scatter_dimension=0, tiled=True)
    backward = pair_sum(back_own, tensor).astype(jnp.bfloat16)
    back_all = lax.all_gather(backward, "dp", axis=0, tiled=True)
    tangent = jnp.dot(inputs_t.T, back_all, preferred_element_type=jnp.float32)
    correlation = lax.psum(matmul(basis_own.T, basis_own), ("dp", "tensor"))
    joint = matmul(jnp.concatenate([basis_own, tangent], axis=1).T, tangent)
    joint, correlation = lax.optimization_barrier((joint, correlation))
    joint = lax.psum(joint, ("dp", "tensor"))
    coupling, square = joint[:rank], joint[rank:]

    cross = matmul(coupling.T, 2.0 * coupling - matmul(correlation, coupling))
    kernel = square - cross
    total = jnp.trace(kernel)
    normed = kernel / total
    vector = leading(normed)
    ratio = jnp.sum(vector * matmul(normed, vector))
    theta = 4.0 * jnp.sqrt(ratio)
    sigma = jnp.sqrt(total * ratio + 1e-06)
    cos_less = jnp.cos(theta) - 1.0
    sine_val = jnp.sin(theta)
    lifted = matmul(coupling, vector)
    left_own = (matmul(tangent, vector) - matmul(basis_own, lifted)) / sigma
    left_low = left_own.astype(jnp.bfloat16)
    probe_part = jnp.dot(inputs_t, left_low, preferred_element_type=jnp.float32)
    probe = lax.psum(probe_part, ("dp", "tensor")).astype(jnp.bfloat16)
    left_part = lax.all_gather(left_own, "dp", axis=0, tiled=True)
    basis_dir = matmul(basis, vector)
    new_basis = basis + jnp.outer(cos_less * basis_dir + sine_val * left_part, vector)
    left_over = (lifted - matmul(correlation.T, lifted)) / sigma
    tilt = cos_less * matmul(correlation.T, vector) + sine_val * left_over
    rotation = correlation + jnp.outer(vector, tilt)

    along = jnp.dot(probe, grads_t, preferred_element_type=jnp.float32)
    lead_row = matmul(vector, grad_proj)
    grad_new = grad_proj + jnp.outer(vector, cos_less * lead_row + sine_val * along)
    first_new = 0.9 * matmul(rotation, first_t) + 0.1 * grad_new
    second_new = 0.95 * matmul(rotation * rotation, second_t) + 0.05 * grad_new * grad_new
    back = jnp.stack(
        [first_new.reshape(dp, rows_own, width), second_new.reshape(dp, rows_own, width)], axis=1
    )
    back = lax.all_to_all(back, "dp", 0, 0, tiled=True)
    back = back.transpose(1, 2, 0, 3).reshape(2, rows_own, dp * width)
    new_first, new_second = back[0], back[1]
    update = new_first / (jnp.sqrt(new_second) + 1e-06)
    return (new_basis, new_first, new_second, update)


def solution(mesh):
    dp, tensor = mesh.shape["dp"], mesh.shape["tensor"]

    def step(*arrays):
        return body(dp, tensor, *arrays)

    return jax.shard_map(
        step,
        mesh=mesh,
        in_specs=(
            P("dp", "tensor"),
            P("dp", "tensor"),
            P("tensor", None),
            P("dp", "tensor"),
            P("dp", "tensor"),
        ),
        out_specs=(P("tensor", None), P("dp", "tensor"), P("dp", "tensor"), P("dp", "tensor")),
        check_vma=False,
    )
```

```python
import functools

import jax
import jax.numpy as jnp
from jax import lax
from jax.experimental import pallas as pl
from jax.experimental.pallas import tpu as pltpu
from jax.sharding import PartitionSpec as P

MESH = pl.DeviceIdType.MESH
VMEM_BYTES = 48 * 1024 * 1024

PI_STEPS = 6


EXACT = lax.Precision.HIGHEST


def matmul(left, right):
    return jnp.dot(left, right, precision=EXACT, preferred_element_type=jnp.float32)


def leading(normed):
    rank_count = normed.shape[0]
    vector = jnp.ones((rank_count,), jnp.float32) / jnp.sqrt(jnp.float32(rank_count))
    for sweep in range(PI_STEPS):
        vector = matmul(normed, vector)
        vector = vector / jnp.sqrt(jnp.sum(vector * vector) + 1e-12)
    return vector


def pair_sum(part, count):
    if count == 2:
        return part + lax.ppermute(part, "tensor", [(0, 1), (1, 0)])
    return lax.psum(part, "tensor")


def exchange_order(dp, tensor):
    bits = lambda name, count: [(name, 1 << b) for b in range(count.bit_length() - 1)]
    along_dp = bits("dp", dp)
    return along_dp[:1] + bits("tensor", tensor) + along_dp[1:]


def sum_kernel(stages, x_ref, o_ref, total, inbox, send_sem, recv_sem):
    pieces = x_ref.shape[0]
    place = {"dp": lax.axis_index("dp"), "tensor": lax.axis_index("tensor")}
    sides, partners = [], []
    for name, bit in stages:
        side = lax.rem(place[name] // bit, 2)
        other = dict(place)
        other[name] = place[name] + bit * (1 - 2 * side)
        sides.append(side)
        partners.append((other["dp"], other["tensor"]))

    barrier = pltpu.get_barrier_semaphore()
    for partner in partners:
        pl.semaphore_signal(barrier, inc=1, device_id=partner, device_id_type=MESH)
    pl.semaphore_wait(barrier, len(stages))

    start, base, half, slot = 0, 0, pieces, 0
    for k, (side, partner) in enumerate(zip(sides, partners)):
        half //= 2
        source = x_ref if k == 0 else total
        keep, give = start + side * half, start + (1 - side) * half
        copy = pltpu.make_async_remote_copy(
            src_ref=source.at[pl.ds(give, half)],
            dst_ref=inbox.at[pl.ds(slot, half)],
            send_sem=send_sem.at[k],
            recv_sem=recv_sem.at[k],
            device_id=partner,
            device_id_type=MESH,
        )
        copy.start()
        copy.wait()
        landing = 0 if k == 0 else keep

        def add(i, carry, source=source, landing=landing, keep=keep, slot=slot):
            total[landing + i] = source[keep + i] + inbox[slot + i]
            return carry

        lax.fori_loop(0, half, add, 0)
        base = base + side * half
        start = landing
        slot += half

    o_ref[base] = total[start].astype(o_ref.dtype)
    size = 1
    for k in reversed(range(len(stages))):
        mine = o_ref.at[pl.ds(base, size)]
        copy = pltpu.make_async_remote_copy(
            src_ref=mine,
            dst_ref=mine,
            send_sem=send_sem.at[len(stages) + k],
            recv_sem=recv_sem.at[len(stages) + k],
            device_id=partners[k],
            device_id_type=MESH,
        )
        copy.start()
        copy.wait()
        base = base - sides[k] * size
        size *= 2


def sum_everywhere(part, kind, dp, tensor, number):
    rows, columns = part.shape
    count = dp * tensor
    stages = exchange_order(dp, tensor)
    block = (rows // count, columns)
    out = pl.pallas_call(
        functools.partial(sum_kernel, stages),
        out_shape=jax.ShapeDtypeStruct((count, *block), kind),
        in_specs=[pl.BlockSpec(memory_space=pltpu.VMEM)],
        out_specs=pl.BlockSpec(memory_space=pltpu.VMEM),
        scratch_shapes=[
            pltpu.VMEM((count // 2, *block), jnp.float32),
            pltpu.VMEM((count - 1, *block), jnp.float32),
            pltpu.SemaphoreType.DMA((2 * len(stages),)),
            pltpu.SemaphoreType.DMA((2 * len(stages),)),
        ],
        compiler_params=pltpu.CompilerParams(
            collective_id=number, has_side_effects=True, vmem_limit_bytes=VMEM_BYTES
        ),
    )(part.reshape(count, *block))
    return out.reshape(rows, columns)


def spread_kernel(dp, tensor, x_ref, o_ref, send_sem, recv_sem):
    count = dp * tensor
    me = lax.axis_index("dp") * tensor + lax.axis_index("tensor")

    def device(index):
        return (index // tensor, lax.rem(index, tensor))

    barrier = pltpu.get_barrier_semaphore()

    def greet(step, carry):
        pl.semaphore_signal(
            barrier, inc=1, device_id=device(lax.rem(me + step, count)), device_id_type=MESH
        )
        return carry

    lax.fori_loop(1, count, greet, 0)
    pl.semaphore_wait(barrier, count - 1)

    def copy(step, place):
        return pltpu.make_async_remote_copy(
            src_ref=x_ref,
            dst_ref=o_ref.at[place],
            send_sem=send_sem.at[step],
            recv_sem=recv_sem.at[step],
            device_id=device(lax.rem(me + step, count)),
            device_id_type=MESH,
        )

    def send(step, carry):
        copy(step, me).start()
        return carry

    def land(step, carry):
        copy(step, lax.rem(me + count - step, count)).wait()
        return carry

    lax.fori_loop(1, count, send, 0)
    o_ref[me] = x_ref[...]
    lax.fori_loop(1, count, land, 0)


def spread(vector, dp, tensor, number):
    count, length = dp * tensor, vector.shape[0]
    rows = -(-length // 1024) * 8
    block = jnp.pad(vector, (0, rows * 128 - length)).reshape(rows, 128)
    out = pl.pallas_call(
        functools.partial(spread_kernel, dp, tensor),
        out_shape=jax.ShapeDtypeStruct((count, rows, 128), jnp.float32),
        in_specs=[pl.BlockSpec(memory_space=pltpu.VMEM)],
        out_specs=pl.BlockSpec(memory_space=pltpu.VMEM),
        scratch_shapes=[
            pltpu.SemaphoreType.DMA((count,)),
            pltpu.SemaphoreType.DMA((count,)),
        ],
        compiler_params=pltpu.CompilerParams(
            collective_id=number, has_side_effects=True, vmem_limit_bytes=VMEM_BYTES
        ),
    )(block)
    return out.reshape(dp, tensor, rows * 128)


def to_columns(block, count):
    rows, columns = block.shape
    pieces = block.reshape(rows, count, columns // count).transpose(1, 0, 2)
    pieces = lax.all_to_all(pieces, "dp", 0, 0, tiled=True)
    return pieces.reshape(count * rows, columns // count)


def body(dp, tensor, layer_inputs, out_grads, basis, first, second):
    rows_own = first.shape[0]
    rank = basis.shape[1]
    feats = basis.shape[0] // dp
    me = lax.axis_index("dp")

    grads_t = to_columns(out_grads, dp)
    basis_low = basis.astype(jnp.bfloat16)
    score_part = jnp.dot(layer_inputs, basis_low, preferred_element_type=jnp.float32)
    scores = pair_sum(score_part, tensor).astype(jnp.bfloat16)
    scores_all = lax.all_gather(scores, "dp", axis=0, tiled=True)
    inputs_t = to_columns(layer_inputs, dp)
    moments = jnp.stack([first, second]).reshape(2, rows_own, dp, -1).transpose(2, 0, 1, 3)
    moments = lax.all_to_all(moments, "dp", 0, 0, tiled=True)
    width = moments.shape[3]
    first_t = moments[:, 0].reshape(rank, width)
    second_t = moments[:, 1].reshape(rank, width)
    basis_own = lax.dynamic_slice_in_dim(basis, me * feats, feats, 0)

    grad_proj = jnp.dot(scores_all.T, grads_t, preferred_element_type=jnp.float32)
    grad_low = grad_proj.astype(jnp.bfloat16)
    back_part = jnp.dot(grads_t, grad_low.T, preferred_element_type=jnp.float32)
    back_all = sum_everywhere(back_part, jnp.bfloat16, dp, tensor, 0)
    tangent = jnp.dot(inputs_t.T, back_all, preferred_element_type=jnp.float32)
    correlation = pair_sum(matmul(basis.T, basis), tensor)
    joint = matmul(jnp.concatenate([basis_own, tangent], axis=1).T, tangent)
    joint = sum_everywhere(joint, jnp.float32, dp, tensor, 1)
    coupling, square = joint[:rank], joint[rank:]

    cross = matmul(coupling.T, 2.0 * coupling - matmul(correlation, coupling))
    kernel = square - cross
    total = jnp.trace(kernel)
    normed = kernel / total
    vector = leading(normed)
    ratio = jnp.sum(vector * matmul(normed, vector))
    theta = 4.0 * jnp.sqrt(ratio)
    sigma = jnp.sqrt(total * ratio + 1e-06)
    cos_less = jnp.cos(theta) - 1.0
    sine_val = jnp.sin(theta)
    lifted = matmul(coupling, vector)
    left_own = (matmul(tangent, vector) - matmul(basis_own, lifted)) / sigma
    left_low = left_own.astype(jnp.bfloat16)
    probe_part = jnp.dot(inputs_t, left_low, preferred_element_type=jnp.float32)
    tokens = probe_part.shape[0]
    parts = spread(jnp.concatenate([probe_part, left_own]), dp, tensor, 2)
    probe = jnp.sum(parts[:, :, :tokens], axis=(0, 1)).astype(jnp.bfloat16)
    left_part = lax.dynamic_index_in_dim(parts, lax.axis_index("tensor"), 1, keepdims=False)
    left_part = left_part[:, tokens : tokens + feats].reshape(-1)
    basis_dir = matmul(basis, vector)
    new_basis = basis + jnp.outer(cos_less * basis_dir + sine_val * left_part, vector)
    left_over = (lifted - matmul(correlation.T, lifted)) / sigma
    tilt = cos_less * matmul(correlation.T, vector) + sine_val * left_over
    rotation = correlation + jnp.outer(vector, tilt)

    along = jnp.dot(probe, grads_t, preferred_element_type=jnp.float32)
    lead_row = matmul(vector, grad_proj)
    grad_new = grad_proj + jnp.outer(vector, cos_less * lead_row + sine_val * along)
    first_new = 0.9 * matmul(rotation, first_t) + 0.1 * grad_new
    second_new = 0.95 * matmul(rotation * rotation, second_t) + 0.05 * grad_new * grad_new
    back = jnp.stack(
        [first_new.reshape(dp, rows_own, width), second_new.reshape(dp, rows_own, width)], axis=1
    )
    back = lax.all_to_all(back, "dp", 0, 0, tiled=True)
    back = back.transpose(1, 2, 0, 3).reshape(2, rows_own, dp * width)
    new_first, new_second = back[0], back[1]
    update = new_first / (jnp.sqrt(new_second) + 1e-06)
    return (new_basis, new_first, new_second, update)


def solution(mesh):
    dp, tensor = mesh.shape["dp"], mesh.shape["tensor"]

    def step(*arrays):
        return body(dp, tensor, *arrays)

    return jax.shard_map(
        step,
        mesh=mesh,
        in_specs=(
            P("dp", "tensor"),
            P("dp", "tensor"),
            P("tensor", None),
            P("dp", "tensor"),
            P("dp", "tensor"),
        ),
        out_specs=(P("tensor", None), P("dp", "tensor"), P("dp", "tensor"), P("dp", "tensor")),
        check_vma=False,
    )
```

```python
import functools

import jax
import jax.numpy as jnp
from jax import lax
from jax.experimental import pallas as pl
from jax.experimental.pallas import tpu as pltpu
from jax.sharding import PartitionSpec as P

MESH = pl.DeviceIdType.MESH
VMEM_BYTES = 48 * 1024 * 1024

PI_STEPS = 6


EXACT = lax.Precision.HIGHEST


def matmul(left, right):
    return jnp.dot(left, right, precision=EXACT, preferred_element_type=jnp.float32)


def leading(normed):
    rank_count = normed.shape[0]
    vector = jnp.ones((rank_count,), jnp.float32) / jnp.sqrt(jnp.float32(rank_count))
    for sweep in range(PI_STEPS):
        vector = matmul(normed, vector)
        vector = vector / jnp.sqrt(jnp.sum(vector * vector) + 1e-12)
    return vector


def pair_sum(part, count):
    if count == 2:
        return part + lax.ppermute(part, "tensor", [(0, 1), (1, 0)])
    return lax.psum(part, "tensor")


def exchange_orders(dp, tensor, groups):
    bits = lambda name, count: [(name, 1 << b) for b in range(count.bit_length() - 1)]
    along_dp = bits("dp", dp)
    rest = bits("tensor", tensor) + along_dp[1:]
    turns = [g * len(rest) // groups for g in range(groups)]
    return [along_dp[:1] + rest[t:] + rest[:t] for t in turns]


def sum_kernel(orders, wire, x_ref, o_ref, total, inbox, outbox, send_sem, recv_sem):
    pieces = x_ref.shape[0]
    width = x_ref.shape[2] // len(orders)
    stages = len(orders[0])
    place = {"dp": lax.axis_index("dp"), "tensor": lax.axis_index("tensor")}
    side, partner = {}, {}
    for name, bit in orders[0]:
        side[name, bit] = lax.rem(place[name] // bit, 2)
        other = dict(place)
        other[name] = place[name] + bit * (1 - 2 * side[name, bit])
        partner[name, bit] = (other["dp"], other["tensor"])

    barrier = pltpu.get_barrier_semaphore()
    for device in partner.values():
        pl.semaphore_signal(barrier, inc=1, device_id=device, device_id_type=MESH)
    pl.semaphore_wait(barrier, stages)

    groups = range(len(orders))
    start, base = [0 for g in groups], [0 for g in groups]
    halves = [pieces >> (k + 1) for k in range(stages)]
    slots = [pieces - (pieces >> k) for k in range(stages)]

    def part(ref, first, size, g):
        return ref.at[pl.ds(first, size), :, pl.ds(g * width, width)]

    def remote(source, target, number, g, stage):
        return pltpu.make_async_remote_copy(
            src_ref=source,
            dst_ref=target,
            send_sem=send_sem.at[g, number],
            recv_sem=recv_sem.at[g, number],
            device_id=partner[stage],
            device_id_type=MESH,
        )

    def give(k, g):
        stage, half = orders[g][k], halves[k]
        source = part(x_ref if k == 0 else total, start[g] + (1 - side[stage]) * half, half, g)
        if wire != jnp.float32:
            staged = part(outbox, slots[k], half, g)
            staged[...] = source[...].astype(wire)
            source = staged
        copy = remote(source, part(inbox, slots[k], half, g), k, g, stage)
        copy.start()
        return copy

    def take(k, g, copy):
        stage, half = orders[g][k], halves[k]
        keep = start[g] + side[stage] * half
        landing = 0 if k == 0 else keep
        copy.wait()
        held = part(x_ref if k == 0 else total, keep, half, g)[...]
        part(total, landing, half, g)[...] = held + part(inbox, slots[k], half, g)[...].astype(
            jnp.float32
        )
        start[g] = landing
        base[g] = base[g] + side[stage] * half

    def hand_on(k, g):
        mine = part(o_ref, base[g], halves[k], g)
        copy = remote(mine, mine, stages + k, g, orders[g][k])
        copy.start()
        return copy

    copies = [give(0, g) for g in groups]
    for k in range(stages):
        for g in groups:
            take(k, g, copies[g])
            if k + 1 < stages:
                copies[g] = give(k + 1, g)
            else:
                part(o_ref, base[g], 1, g)[...] = part(total, start[g], 1, g)[...].astype(o_ref.dtype)
                copies[g] = hand_on(k, g)
    for k in reversed(range(stages)):
        for g in groups:
            copies[g].wait()
            base[g] = base[g] - side[orders[g][k]] * halves[k]
            if k > 0:
                copies[g] = hand_on(k - 1, g)


def sum_everywhere(part, kind, wire, dp, tensor, number):
    rows, columns = part.shape
    count = dp * tensor
    orders = exchange_orders(dp, tensor, 4)
    stages = len(orders[0])
    block = (rows // count, columns)
    out = pl.pallas_call(
        functools.partial(sum_kernel, orders, wire),
        out_shape=jax.ShapeDtypeStruct((count, *block), kind),
        in_specs=[pl.BlockSpec(memory_space=pltpu.VMEM)],
        out_specs=pl.BlockSpec(memory_space=pltpu.VMEM),
        scratch_shapes=[
            pltpu.VMEM((count // 2, *block), jnp.float32),
            pltpu.VMEM((count - 1, *block), wire),
            pltpu.VMEM((1 if wire == jnp.float32 else count - 1, *block), wire),
            pltpu.SemaphoreType.DMA((4, 2 * stages)),
            pltpu.SemaphoreType.DMA((4, 2 * stages)),
        ],
        compiler_params=pltpu.CompilerParams(
            collective_id=number, has_side_effects=True, vmem_limit_bytes=VMEM_BYTES
        ),
    )(part.reshape(count, *block))
    return out.reshape(rows, columns)


def spread_kernel(dp, tensor, x_ref, o_ref, send_sem, recv_sem):
    count = dp * tensor
    me = lax.axis_index("dp") * tensor + lax.axis_index("tensor")

    def device(index):
        return (index // tensor, lax.rem(index, tensor))

    barrier = pltpu.get_barrier_semaphore()

    def greet(step, carry):
        pl.semaphore_signal(
            barrier, inc=1, device_id=device(lax.rem(me + step, count)), device_id_type=MESH
        )
        return carry

    lax.fori_loop(1, count, greet, 0)
    pl.semaphore_wait(barrier, count - 1)

    def copy(step, place):
        return pltpu.make_async_remote_copy(
            src_ref=x_ref,
            dst_ref=o_ref.at[place],
            send_sem=send_sem.at[step],
            recv_sem=recv_sem.at[step],
            device_id=device(lax.rem(me + step, count)),
            device_id_type=MESH,
        )

    def send(step, carry):
        copy(step, me).start()
        return carry

    def land(step, carry):
        copy(step, lax.rem(me + count - step, count)).wait()
        return carry

    lax.fori_loop(1, count, send, 0)
    o_ref[me] = x_ref[...]
    lax.fori_loop(1, count, land, 0)


def spread(vector, dp, tensor, number):
    count, length = dp * tensor, vector.shape[0]
    rows = -(-length // 1024) * 8
    block = jnp.pad(vector, (0, rows * 128 - length)).reshape(rows, 128)
    out = pl.pallas_call(
        functools.partial(spread_kernel, dp, tensor),
        out_shape=jax.ShapeDtypeStruct((count, rows, 128), jnp.float32),
        in_specs=[pl.BlockSpec(memory_space=pltpu.VMEM)],
        out_specs=pl.BlockSpec(memory_space=pltpu.VMEM),
        scratch_shapes=[
            pltpu.SemaphoreType.DMA((count,)),
            pltpu.SemaphoreType.DMA((count,)),
        ],
        compiler_params=pltpu.CompilerParams(
            collective_id=number, has_side_effects=True, vmem_limit_bytes=VMEM_BYTES
        ),
    )(block)
    return out.reshape(dp, tensor, rows * 128)


def to_columns(block, count):
    rows, columns = block.shape
    pieces = block.reshape(rows, count, columns // count).transpose(1, 0, 2)
    pieces = lax.all_to_all(pieces, "dp", 0, 0, tiled=True)
    return pieces.reshape(count * rows, columns // count)


def body(dp, tensor, layer_inputs, out_grads, basis, first, second):
    rows_own = first.shape[0]
    rank = basis.shape[1]
    feats = basis.shape[0] // dp
    me = lax.axis_index("dp")

    grads_t = to_columns(out_grads, dp)
    basis_low = basis.astype(jnp.bfloat16)
    score_part = jnp.dot(layer_inputs, basis_low, preferred_element_type=jnp.float32)
    scores = pair_sum(score_part, tensor).astype(jnp.bfloat16)
    scores_all = lax.all_gather(scores, "dp", axis=0, tiled=True)
    layer_inputs, grads_t = lax.optimization_barrier((layer_inputs, grads_t))
    inputs_t = to_columns(layer_inputs, dp)
    first, second, inputs_t = lax.optimization_barrier((first, second, inputs_t))
    moments = jnp.stack([first, second]).reshape(2, rows_own, dp, -1).transpose(2, 0, 1, 3)
    moments = lax.all_to_all(moments, "dp", 0, 0, tiled=True)
    width = moments.shape[3]
    first_t = moments[:, 0].reshape(rank, width)
    second_t = moments[:, 1].reshape(rank, width)
    basis_own = lax.dynamic_slice_in_dim(basis, me * feats, feats, 0)

    grad_proj = jnp.dot(scores_all.T, grads_t, preferred_element_type=jnp.float32)
    grad_low = grad_proj.astype(jnp.bfloat16)
    back_part = jnp.dot(grads_t, grad_low.T, preferred_element_type=jnp.float32)
    back_all = sum_everywhere(back_part, jnp.bfloat16, jnp.bfloat16, dp, tensor, 0)
    tangent = jnp.dot(inputs_t.T, back_all, preferred_element_type=jnp.float32)
    correlation = pair_sum(matmul(basis.T, basis), tensor)
    joint = matmul(jnp.concatenate([basis_own, tangent], axis=1).T, tangent)
    joint = sum_everywhere(joint, jnp.float32, jnp.float32, dp, tensor, 1)
    coupling, square = joint[:rank], joint[rank:]

    cross = matmul(coupling.T, 2.0 * coupling - matmul(correlation, coupling))
    kernel = square - cross
    total = jnp.trace(kernel)
    normed = kernel / total
    vector = leading(normed)
    ratio = jnp.sum(vector * matmul(normed, vector))
    theta = 4.0 * jnp.sqrt(ratio)
    sigma = jnp.sqrt(total * ratio + 1e-06)
    cos_less = jnp.cos(theta) - 1.0
    sine_val = jnp.sin(theta)
    lifted = matmul(coupling, vector)
    left_own = (matmul(tangent, vector) - matmul(basis_own, lifted)) / sigma
    left_low = left_own.astype(jnp.bfloat16)
    probe_part = jnp.dot(inputs_t, left_low, preferred_element_type=jnp.float32)
    tokens = probe_part.shape[0]
    parts = spread(jnp.concatenate([probe_part, left_own]), dp, tensor, 2)
    probe = jnp.sum(parts[:, :, :tokens], axis=(0, 1)).astype(jnp.bfloat16)
    left_part = lax.dynamic_index_in_dim(parts, lax.axis_index("tensor"), 1, keepdims=False)
    left_part = left_part[:, tokens : tokens + feats].reshape(-1)
    basis_dir = matmul(basis, vector)
    new_basis = basis + jnp.outer(cos_less * basis_dir + sine_val * left_part, vector)
    left_over = (lifted - matmul(correlation.T, lifted)) / sigma
    tilt = cos_less * matmul(correlation.T, vector) + sine_val * left_over
    rotation = correlation + jnp.outer(vector, tilt)

    along = jnp.dot(probe, grads_t, preferred_element_type=jnp.float32)
    lead_row = matmul(vector, grad_proj)
    grad_new = grad_proj + jnp.outer(vector, cos_less * lead_row + sine_val * along)
    first_new = 0.9 * matmul(rotation, first_t) + 0.1 * grad_new
    second_new = 0.95 * matmul(rotation * rotation, second_t) + 0.05 * grad_new * grad_new
    back = jnp.stack(
        [first_new.reshape(dp, rows_own, width), second_new.reshape(dp, rows_own, width)], axis=1
    )
    back = lax.all_to_all(back, "dp", 0, 0, tiled=True)
    back = back.transpose(1, 2, 0, 3).reshape(2, rows_own, dp * width)
    new_first, new_second = back[0], back[1]
    update = new_first / (jnp.sqrt(new_second) + 1e-06)
    return (new_basis, new_first, new_second, update)


def solution(mesh):
    dp, tensor = mesh.shape["dp"], mesh.shape["tensor"]

    def step(*arrays):
        return body(dp, tensor, *arrays)

    return jax.shard_map(
        step,
        mesh=mesh,
        in_specs=(
            P("dp", "tensor"),
            P("dp", "tensor"),
            P("tensor", None),
            P("dp", "tensor"),
            P("dp", "tensor"),
        ),
        out_specs=(P("tensor", None), P("dp", "tensor"), P("dp", "tensor"), P("dp", "tensor")),
        check_vma=False,
    )
```

```python
import functools

import jax
import jax.numpy as jnp
from jax import lax
from jax.experimental import pallas as pl
from jax.experimental.pallas import tpu as pltpu
from jax.sharding import PartitionSpec as P

MESH = pl.DeviceIdType.MESH
VMEM_BYTES = 48 * 1024 * 1024

PI_STEPS = 6


EXACT = lax.Precision.HIGHEST


def matmul(left, right):
    return jnp.dot(left, right, precision=EXACT, preferred_element_type=jnp.float32)


def leading(normed):
    rank_count = normed.shape[0]
    vector = jnp.ones((rank_count,), jnp.float32) / jnp.sqrt(jnp.float32(rank_count))
    for sweep in range(PI_STEPS):
        vector = matmul(normed, vector)
        vector = vector / jnp.sqrt(jnp.sum(vector * vector) + 1e-12)
    return vector


def pair_sum(part, count):
    if count == 2:
        return part + lax.ppermute(part, "tensor", [(0, 1), (1, 0)])
    return lax.psum(part, "tensor")


def exchange_orders(dp, tensor, groups):
    bits = lambda name, count: [(name, 1 << b) for b in range(count.bit_length() - 1)]
    along_dp = bits("dp", dp)
    rest = bits("tensor", tensor) + along_dp[1:]
    turns = [g * len(rest) // groups for g in range(groups)]
    return [along_dp[:1] + rest[t:] + rest[:t] for t in turns]


def sum_kernel(orders, wire, x_ref, o_ref, total, inbox, outbox, send_sem, recv_sem):
    pieces = x_ref.shape[0]
    width = x_ref.shape[2] // len(orders)
    stages = len(orders[0])
    place = {"dp": lax.axis_index("dp"), "tensor": lax.axis_index("tensor")}
    side, partner = {}, {}
    for name, bit in orders[0]:
        side[name, bit] = lax.rem(place[name] // bit, 2)
        other = dict(place)
        other[name] = place[name] + bit * (1 - 2 * side[name, bit])
        partner[name, bit] = (other["dp"], other["tensor"])

    barrier = pltpu.get_barrier_semaphore()
    for device in partner.values():
        pl.semaphore_signal(barrier, inc=1, device_id=device, device_id_type=MESH)
    pl.semaphore_wait(barrier, stages)

    groups = range(len(orders))
    start, base = [0 for g in groups], [0 for g in groups]
    halves = [pieces >> (k + 1) for k in range(stages)]
    slots = [pieces - (pieces >> k) for k in range(stages)]

    def part(ref, first, size, g):
        return ref.at[pl.ds(first, size), :, pl.ds(g * width, width)]

    def remote(source, target, number, g, stage):
        return pltpu.make_async_remote_copy(
            src_ref=source,
            dst_ref=target,
            send_sem=send_sem.at[g, number],
            recv_sem=recv_sem.at[g, number],
            device_id=partner[stage],
            device_id_type=MESH,
        )

    def give(k, g):
        stage, half = orders[g][k], halves[k]
        source = part(x_ref if k == 0 else total, start[g] + (1 - side[stage]) * half, half, g)
        if wire != jnp.float32:
            staged = part(outbox, slots[k], half, g)
            staged[...] = source[...].astype(wire)
            source = staged
        copy = remote(source, part(inbox, slots[k], half, g), k, g, stage)
        copy.start()
        return copy

    def take(k, g, copy):
        stage, half = orders[g][k], halves[k]
        keep = start[g] + side[stage] * half
        landing = 0 if k == 0 else keep
        copy.wait()
        held = part(x_ref if k == 0 else total, keep, half, g)[...]
        part(total, landing, half, g)[...] = held + part(inbox, slots[k], half, g)[...].astype(
            jnp.float32
        )
        start[g] = landing
        base[g] = base[g] + side[stage] * half

    def hand_on(k, g):
        mine = part(o_ref, base[g], halves[k], g)
        copy = remote(mine, mine, stages + k, g, orders[g][k])
        copy.start()
        return copy

    copies = [give(0, g) for g in groups]
    for k in range(stages):
        for g in groups:
            take(k, g, copies[g])
            if k + 1 < stages:
                copies[g] = give(k + 1, g)
            else:
                part(o_ref, base[g], 1, g)[...] = part(total, start[g], 1, g)[...].astype(o_ref.dtype)
                copies[g] = hand_on(k, g)
    for k in reversed(range(stages)):
        for g in groups:
            copies[g].wait()
            base[g] = base[g] - side[orders[g][k]] * halves[k]
            if k > 0:
                copies[g] = hand_on(k - 1, g)


def sum_everywhere(part, kind, wire, dp, tensor, number):
    rows, columns = part.shape
    count = dp * tensor
    orders = exchange_orders(dp, tensor, 4)
    stages = len(orders[0])
    block = (rows // count, columns)
    out = pl.pallas_call(
        functools.partial(sum_kernel, orders, wire),
        out_shape=jax.ShapeDtypeStruct((count, *block), kind),
        in_specs=[pl.BlockSpec(memory_space=pltpu.VMEM)],
        out_specs=pl.BlockSpec(memory_space=pltpu.VMEM),
        scratch_shapes=[
            pltpu.VMEM((count // 2, *block), jnp.float32),
            pltpu.VMEM((count - 1, *block), wire),
            pltpu.VMEM((1 if wire == jnp.float32 else count - 1, *block), wire),
            pltpu.SemaphoreType.DMA((4, 2 * stages)),
            pltpu.SemaphoreType.DMA((4, 2 * stages)),
        ],
        compiler_params=pltpu.CompilerParams(
            collective_id=number, has_side_effects=True, vmem_limit_bytes=VMEM_BYTES
        ),
    )(part.reshape(count, *block))
    return out.reshape(rows, columns)


def spread_kernel(dp, tensor, x_ref, o_ref, send_sem, recv_sem):
    count = dp * tensor
    me = lax.axis_index("dp") * tensor + lax.axis_index("tensor")

    def device(index):
        return (index // tensor, lax.rem(index, tensor))

    barrier = pltpu.get_barrier_semaphore()

    def greet(step, carry):
        pl.semaphore_signal(
            barrier, inc=1, device_id=device(lax.rem(me + step, count)), device_id_type=MESH
        )
        return carry

    lax.fori_loop(1, count, greet, 0)
    pl.semaphore_wait(barrier, count - 1)

    def copy(step, place):
        return pltpu.make_async_remote_copy(
            src_ref=x_ref,
            dst_ref=o_ref.at[place],
            send_sem=send_sem.at[step],
            recv_sem=recv_sem.at[step],
            device_id=device(lax.rem(me + step, count)),
            device_id_type=MESH,
        )

    def send(step, carry):
        copy(step, me).start()
        return carry

    def land(step, carry):
        copy(step, lax.rem(me + count - step, count)).wait()
        return carry

    lax.fori_loop(1, count, send, 0)
    o_ref[me] = x_ref[...]
    lax.fori_loop(1, count, land, 0)


def spread(vector, dp, tensor, number):
    count, length = dp * tensor, vector.shape[0]
    rows = -(-length // 1024) * 8
    block = jnp.pad(vector, (0, rows * 128 - length)).reshape(rows, 128)
    out = pl.pallas_call(
        functools.partial(spread_kernel, dp, tensor),
        out_shape=jax.ShapeDtypeStruct((count, rows, 128), jnp.float32),
        in_specs=[pl.BlockSpec(memory_space=pltpu.VMEM)],
        out_specs=pl.BlockSpec(memory_space=pltpu.VMEM),
        scratch_shapes=[
            pltpu.SemaphoreType.DMA((count,)),
            pltpu.SemaphoreType.DMA((count,)),
        ],
        compiler_params=pltpu.CompilerParams(
            collective_id=number, has_side_effects=True, vmem_limit_bytes=VMEM_BYTES
        ),
    )(block)
    return out.reshape(dp, tensor, rows * 128)


def to_columns(block, count):
    rows, columns = block.shape
    pieces = block.reshape(rows, count, columns // count).transpose(1, 0, 2)
    pieces = lax.all_to_all(pieces, "dp", 0, 0, tiled=True)
    return pieces.reshape(count * rows, columns // count)


def body(dp, tensor, layer_inputs, out_grads, basis, first, second):
    rows_own = first.shape[0]
    rank = basis.shape[1]
    feats = basis.shape[0] // dp
    me = lax.axis_index("dp")

    grads_t = to_columns(out_grads, dp)
    basis_low = basis.astype(jnp.bfloat16)
    score_part = jnp.dot(layer_inputs, basis_low, preferred_element_type=jnp.float32)
    scores = pair_sum(score_part, tensor).astype(jnp.bfloat16)
    scores_all = lax.all_gather(scores, "dp", axis=0, tiled=True)
    layer_inputs, grads_t = lax.optimization_barrier((layer_inputs, grads_t))
    inputs_t = to_columns(layer_inputs, dp)
    first, second, inputs_t = lax.optimization_barrier((first, second, inputs_t))
    moments = jnp.stack([first, second]).reshape(2, rows_own, dp, -1).transpose(2, 0, 1, 3)
    moments = lax.all_to_all(moments, "dp", 0, 0, tiled=True)
    width = moments.shape[3]
    first_t = moments[:, 0].reshape(rank, width)
    second_t = moments[:, 1].reshape(rank, width)
    basis_own = lax.dynamic_slice_in_dim(basis, me * feats, feats, 0)

    grad_proj = jnp.dot(scores_all.T, grads_t, preferred_element_type=jnp.float32)
    grad_low = grad_proj.astype(jnp.bfloat16)
    back_part = jnp.dot(grads_t, grad_low.T, preferred_element_type=jnp.float32)
    back_all = sum_everywhere(back_part, jnp.bfloat16, jnp.bfloat16, dp, tensor, 0)
    tangent = jnp.dot(inputs_t.T, back_all, preferred_element_type=jnp.float32)
    joint = matmul(jnp.concatenate([basis_own, tangent], axis=1).T, tangent)
    joint = jnp.concatenate([joint, matmul(basis_own.T, basis_own)], axis=0)
    joint = sum_everywhere(joint, jnp.float32, jnp.float32, dp, tensor, 1)
    coupling, square, correlation = joint[:rank], joint[rank : 2 * rank], joint[2 * rank :]

    cross = matmul(coupling.T, 2.0 * coupling - matmul(correlation, coupling))
    kernel = square - cross
    total = jnp.trace(kernel)
    normed = kernel / total
    vector = leading(normed)
    ratio = jnp.sum(vector * matmul(normed, vector))
    theta = 4.0 * jnp.sqrt(ratio)
    sigma = jnp.sqrt(total * ratio + 1e-06)
    cos_less = jnp.cos(theta) - 1.0
    sine_val = jnp.sin(theta)
    lifted = matmul(coupling, vector)
    left_own = (matmul(tangent, vector) - matmul(basis_own, lifted)) / sigma
    left_low = left_own.astype(jnp.bfloat16)
    probe_part = jnp.dot(inputs_t, left_low, preferred_element_type=jnp.float32)
    tokens = probe_part.shape[0]
    parts = spread(jnp.concatenate([probe_part, left_own]), dp, tensor, 2)
    probe = jnp.sum(parts[:, :, :tokens], axis=(0, 1)).astype(jnp.bfloat16)
    left_part = lax.dynamic_index_in_dim(parts, lax.axis_index("tensor"), 1, keepdims=False)
    left_part = left_part[:, tokens : tokens + feats].reshape(-1)
    basis_dir = matmul(basis, vector)
    new_basis = basis + jnp.outer(cos_less * basis_dir + sine_val * left_part, vector)
    left_over = (lifted - matmul(correlation.T, lifted)) / sigma
    tilt = cos_less * matmul(correlation.T, vector) + sine_val * left_over
    rotation = correlation + jnp.outer(vector, tilt)

    along = jnp.dot(probe, grads_t, preferred_element_type=jnp.float32)
    lead_row = matmul(vector, grad_proj)
    grad_new = grad_proj + jnp.outer(vector, cos_less * lead_row + sine_val * along)
    first_new = 0.9 * matmul(rotation, first_t) + 0.1 * grad_new
    second_new = 0.95 * matmul(rotation * rotation, second_t) + 0.05 * grad_new * grad_new
    back = jnp.stack(
        [first_new.reshape(dp, rows_own, width), second_new.reshape(dp, rows_own, width)], axis=1
    )
    back = lax.all_to_all(back, "dp", 0, 0, tiled=True)
    back = back.transpose(1, 2, 0, 3).reshape(2, rows_own, dp * width)
    new_first, new_second = back[0], back[1]
    update = new_first / (jnp.sqrt(new_second) + 1e-06)
    return (new_basis, new_first, new_second, update)


def solution(mesh):
    dp, tensor = mesh.shape["dp"], mesh.shape["tensor"]

    def step(*arrays):
        return body(dp, tensor, *arrays)

    return jax.shard_map(
        step,
        mesh=mesh,
        in_specs=(
            P("dp", "tensor"),
            P("dp", "tensor"),
            P("tensor", None),
            P("dp", "tensor"),
            P("dp", "tensor"),
        ),
        out_specs=(P("tensor", None), P("dp", "tensor"), P("dp", "tensor"), P("dp", "tensor")),
        check_vma=False,
    )
```
